32 devices in a mesh: gx: 4 (over z), gy: 4 (over y, x), gz: 2 (over core).
Axes of the slice: x: 2, y: 2, z: 4, core: 2. Of those that a mesh axis runs over, the one named last changes fastest.
Arguments:
- coeffs: float32 [5, 5, 5, 5, 512], P(None, None, None, None, ('gx', 'gy', 'gz')), may hold values from -6 to 6
- refine_flag: int32 [512], P(('gx', 'gy', 'gz')), may hold values from 0 to 1, as said below
- new_owner: int32 [512], P(('gx', 'gy', 'gz')), may hold values from 0 to 31, as said below
- inv_jac: float32 [5, 5, 5, 8192], P(None, None, None, ('gx', 'gy', 'gz')), may hold values from 0.02 to 0.2
- metric: float32 [3, 3, 5, 5, 5, 8192], P(None, None, None, None, None, ('gx', 'gy', 'gz')), may hold values from -3 to 3
- neighbor: int32 [4, 6, 8192], P(None, None, ('gx', 'gy', 'gz')), may hold values from 0 to 2047, as said below
- mortar: int32 [6, 8192], P(None, ('gx', 'gy', 'gz')), may hold values from 0 to 5, as said below
- export_up: int32 [8192], P(('gx', 'gy', 'gz')), may hold values from 0 to 1535, as said below
- export_down: int32 [8192], P(('gx', 'gy', 'gz')), may hold values from 0 to 1535, as said below
Outputs:
- rhs: float32 [5, 5, 5, 5, 8192], P(None, None, None, None, ('gx', 'gy', 'gz'))
The draws below stay inside these ranges and needn't reach their ends.
Inputs may be any that keep to these rules, and one draw needn't show every extreme that they name: `new_owner`: device s keeps a middle run of its parents and sends a run at the head of its segment to devices s - 2 and s - 1 (the first parents to s - 2) and a run at the tail to s + 1 and s + 2 (the last parents to s + 2); no parent leaves the devices 0 to 32 - 1; at most 4 parents go from one device to one other device, and some device sends exactly 4 to each of s - 2, s - 1, s + 1, s + 2. `refine_flag`: the share of refined parents differs from device to device. `neighbor`: entries of used element slots name traces of used slots or halo entries; a slot that holds no element has kind 0; slots that a face's kind does not read hold any index. `mortar`: slots that hold no element have kind 0. `export_up`: entries name traces of used element slots. `export_down`: entries name traces of used element slots.
All inputs are finite; a program needn't handle non-finite values.
Results may differ from the reference program's by a relative error of at most 0.0003.
Values sent between devices are 32-bit elements; how exact they have to be, the bound alone decides.
A program may use at most 320 MiB of HBM per device.

```python
import math
import jax
import jax.numpy as jnp
import numpy as np
from jax import lax

VARS = 5
ORDER = 4
NP = 5
ELEM_DEV = 16
HALO = 256
RANKS = 32
CAP = 4
PARENT_SLOTS = 32
ELEM_NEW = 256
ELEMS = 512
ELEMS_NEW = 8192


def layout(key):
    level = jax.random.randint(jax.random.fold_in(key, 101), (RANKS, 1), 1, 8)
    raw = jax.random.randint(jax.random.fold_in(key, 102), (RANKS, ELEM_DEV), 0, 8)
    flags = (raw < level).astype(jnp.int32)
    sources = jnp.arange(RANKS, dtype=jnp.int32)[:, None]
    runs = jax.random.randint(jax.random.fold_in(key, 103), (RANKS, 4), 0, CAP + 1)
    runs = runs.at[2].set(CAP)
    reach = jnp.array([-2, -1, 1, 2], jnp.int32)[None, :]
    inside = (sources + reach >= 0) & (sources + reach < RANKS)
    runs = jnp.where(inside, runs, 0).astype(jnp.int32)
    position = jnp.arange(ELEM_DEV, dtype=jnp.int32)[None, :]
    far_down, near_down, near_up, far_up = (runs[:, 0:1], runs[:, 1:2], runs[:, 2:3], runs[:, 3:4])
    owners = sources + jnp.zeros_like(position)
    owners = jnp.where(position < far_down + near_down, sources - 1, owners)
    owners = jnp.where(position < far_down, sources - 2, owners)
    owners = jnp.where(position >= ELEM_DEV - far_up - near_up, sources + 1, owners)
    owners = jnp.where(position >= ELEM_DEV - far_up, sources + 2, owners)
    owners = owners.astype(jnp.int32)
    same = owners[:, :, None] == owners[:, None, :]
    earlier = position[:, None, :] < position[:, :, None]
    slot = jnp.sum((same & earlier).astype(jnp.int32), axis=-1)
    delta = owners - sources
    kept = 2 * CAP + position
    upper = (2 - delta) * CAP + slot
    lower = 2 * CAP + ELEM_DEV + (-delta - 1) * CAP + slot
    spot = jnp.where(delta == 0, kept, jnp.where(delta > 0, upper, lower))
    target = (owners * PARENT_SLOTS + spot).reshape(-1)
    occupied = jnp.zeros((RANKS * ELEM_NEW,), jnp.int32)
    flat_flags = flags.reshape(-1)
    for child in range(8):
        marks = flat_flags if child > 0 else jnp.ones_like(flat_flags)
        occupied = occupied.at[target * 8 + child].max(marks)
    return (flags, owners, occupied.reshape(RANKS, ELEM_NEW))


def pick_faces(key, occupied, shape):
    order = jnp.argsort(1 - occupied, axis=1, stable=True)
    filled = jnp.sum(occupied, axis=1)
    total = 1
    for extent in shape:
        total = total * extent
    ranks_picked = jax.random.randint(jax.random.fold_in(key, 1), (RANKS, total), 0, filled[:, None])
    elements = jnp.take_along_axis(order, ranks_picked, axis=1)
    faces = jax.random.randint(jax.random.fold_in(key, 2), (RANKS, total), 0, 6)
    return (faces * ELEM_NEW + elements).astype(jnp.int32).reshape((RANKS,) + shape)


def draw_refine_flag(key, part):
    flags, owners, occupied = layout(key)
    return flags.reshape(-1)


def draw_new_owner(key, part):
    flags, owners, occupied = layout(key)
    return owners.reshape(-1)


def draw_neighbor(key, part):
    flags, owners, occupied = layout(key)
    shape = (4, 6, ELEM_NEW)
    local = pick_faces(jax.random.fold_in(key, 201), occupied, shape)
    remote = 6 * ELEM_NEW + jax.random.randint(jax.random.fold_in(key, 202), (RANKS,) + shape, 0, 2 * HALO)
    use_remote = jax.random.randint(jax.random.fold_in(key, 203), (RANKS,) + shape, 0, 100) < 15
    chosen = jnp.where(use_remote, remote, local)
    own = jnp.arange(6, dtype=jnp.int32)[:, None] * ELEM_NEW + jnp.arange(ELEM_NEW, dtype=jnp.int32)[None, :]
    own = jnp.broadcast_to(own[None, None], (RANKS,) + shape)
    chosen = jnp.where(occupied[:, None, None, :] > 0, chosen, own)
    chosen = chosen.at[:, 0, 0, 0].set(6 * ELEM_NEW + 2 * HALO - 1)
    chosen = chosen.at[:, 1, 0, 0].set(0)
    return jnp.moveaxis(chosen, 0, 2).reshape(4, 6, RANKS * ELEM_NEW).astype(jnp.int32)


def draw_mortar(key, part):
    flags, owners, occupied = layout(key)
    shape = (RANKS, 6, ELEM_NEW)
    roll = jax.random.randint(jax.random.fold_in(key, 301), shape, 0, 10)
    quarter = jax.random.randint(jax.random.fold_in(key, 302), shape, 1, 5)
    kinds = jnp.where(roll < 6, 0, jnp.where(roll < 8, quarter, 5))
    kinds = jnp.where(occupied[:, None, :] > 0, kinds, 0)
    kinds = kinds.at[:, 0, 0].set(0)
    return jnp.moveaxis(kinds, 0, 1).reshape(6, RANKS * ELEM_NEW).astype(jnp.int32)


def draw_export_up(key, part):
    flags, owners, occupied = layout(key)
    return pick_faces(jax.random.fold_in(key, 401), occupied, (HALO,)).reshape(-1)


def draw_export_down(key, part):
    flags, owners, occupied = layout(key)
    return pick_faces(jax.random.fold_in(key, 402), occupied, (HALO,)).reshape(-1)


def level_of(stream_key, shape, cuts, low, high):
    factor_of, own = 1.0, jax.random.fold_in(stream_key, 6)
    for axis_at, shards_of in cuts:
        draws = jnp.exp(jax.random.uniform(jax.random.fold_in(own, axis_at), (shards_of,), jnp.float32, low / len(cuts), high / len(cuts)))
        factor_of = factor_of * jnp.repeat(draws, shape[axis_at] // shards_of).reshape([-1 if axis == axis_at else 1 for axis in range(len(shape))])
    return factor_of


def scatter_about(rng, shape, spread, bound, split=(), kind=jnp.bfloat16):
    entries = spread * jax.random.normal(rng, shape, jnp.float32)
    if split:
        entries = entries * level_of(rng, shape, split, -0.22, 0.18)
    return jnp.clip(entries, -bound, bound).astype(kind)


def setup_inputs(seed: int = 0) -> dict:
    streams_of = jax.random.split(jax.random.key(seed), 10)
    return {
        "coeffs": scatter_about(streams_of[0], (VARS, NP, NP, NP, ELEMS), 1.0, 6.0, ((4, 32),), jnp.float32),
        "refine_flag": draw_refine_flag(jax.random.fold_in(streams_of[9], 71), 0),
        "new_owner": draw_new_owner(jax.random.fold_in(streams_of[9], 71), 0),
        "inv_jac": jnp.clip(jnp.exp(math.log(0.2) - 2.3025851 * jax.random.uniform(streams_of[3], (NP, NP, NP, ELEMS_NEW), jnp.float32) ** level_of(streams_of[3], (NP, NP, NP, ELEMS_NEW), ((3, 32),), -0.2, 0.2)), 0.02, 0.2),
        "metric": scatter_about(streams_of[4], (3, 3, NP, NP, NP, ELEMS_NEW), 0.5, 3.0, ((5, 32),), jnp.float32),
        "neighbor": draw_neighbor(jax.random.fold_in(streams_of[9], 71), 0),
        "mortar": draw_mortar(jax.random.fold_in(streams_of[9], 71), 0),
        "export_up": draw_export_up(jax.random.fold_in(streams_of[9], 71), 0),
        "export_down": draw_export_down(jax.random.fold_in(streams_of[9], 71), 0),
    }


HIGHEST = lax.Precision.HIGHEST
mean_flow = (0.5, 0.3, 0.2)
speed_bound = 1.5


def lobatto_rule(degree):
    count = degree + 1
    nodes = np.cos(np.pi * np.arange(count) / degree)
    table = np.zeros((count, count))
    for sweep in range(80):
        table[:, 0] = 1.0
        table[:, 1] = nodes
        for power in range(2, count):
            table[:, power] = ((2 * power - 1) * nodes * table[:, power - 1] - (power - 1) * table[:, power - 2]) / power
        nodes = nodes - (nodes * table[:, degree] - table[:, degree - 1]) / (count * table[:, degree])
    table[:, 0] = 1.0
    table[:, 1] = nodes
    for power in range(2, count):
        table[:, power] = ((2 * power - 1) * nodes * table[:, power - 1] - (power - 1) * table[:, power - 2]) / power
    weights = 2.0 / (degree * count * table[:, degree] ** 2)
    return np.array(nodes[::-1]), np.array(weights[::-1])


def node_tables():
    degree = ORDER
    count = degree + 1
    nodes, weights = lobatto_rule(degree)
    bary = np.array([1.0 / np.prod([nodes[k] - nodes[other] for other in range(count) if other != k]) for k in range(count)])
    deriv = np.zeros((count, count))
    for row in range(count):
        for column in range(count):
            if row != column:
                deriv[row, column] = bary[column] / bary[row] / (nodes[row] - nodes[column])
        deriv[row, row] = -np.sum(deriv[row])
    interp = np.zeros((2, count, count))
    for half in range(2):
        points = (nodes + 2.0 * half - 1.0) / 2.0
        for column in range(count):
            value = np.ones(count)
            for other in range(count):
                if other != column:
                    value = value * (points - nodes[other]) / (nodes[column] - nodes[other])
            interp[half, :, column] = value
    project = 0.5 * np.transpose(interp, (0, 2, 1)) * weights[None, None, :] / weights[None, :, None]
    return (jnp.asarray(deriv, jnp.float32), jnp.asarray(interp, jnp.float32),
            jnp.asarray(project, jnp.float32), float(1.0 / weights[0]))


def refine_elements(parents, refined, interp):
    children = []
    for child in range(8):
        first, second, third = child // 4, (child // 2) % 2, child % 2
        section = jnp.einsum('ak,vklme->valme', interp[first], parents, precision=HIGHEST)
        section = jnp.einsum('bl,valme->vabme', interp[second], section, precision=HIGHEST)
        section = jnp.einsum('cm,vabme->vabce', interp[third], section, precision=HIGHEST)
        if child == 0:
            section = jnp.where(refined, section, parents)
        else:
            section = jnp.where(refined, section, jnp.zeros_like(section))
        children.append(section)
    stacked = jnp.stack(children, axis=-1)
    return stacked.reshape(stacked.shape[:-2] + (stacked.shape[-2] * 8,))


def normal_flux(rows, state):
    along = rows[0] * state[1] + rows[1] * state[2] + rows[2] * state[3]
    carried = mean_flow[0] * rows[0] + mean_flow[1] * rows[1] + mean_flow[2] * rows[2]
    parts = [carried * state[0] + along]
    for direction in range(3):
        parts.append(carried * state[1 + direction] + rows[direction] * state[4])
    parts.append(carried * state[4] + along)
    return jnp.stack(parts)


def face_parts(array):
    return [array[:, 0], array[:, -1], array[:, :, 0], array[:, :, -1], array[:, :, :, 0], array[:, :, :, -1]]


def face_traces(state):
    return jnp.concatenate(face_parts(state), axis=-1)


def apply_pair(left, right, traces):
    section = jnp.einsum('ak,vkle->vale', left, traces, precision=HIGHEST)
    return jnp.einsum('bl,vale->vabe', right, section, precision=HIGHEST)


def right_side(state, metric, inv_jac, neighbor, mortar, traces, before, after, tables):
    deriv, interp, project, lift_scale = tables
    count = state.shape[-1]
    volume = jnp.einsum('al,vlbce->vabce', deriv, normal_flux(metric[0], state), precision=HIGHEST)
    volume = volume + jnp.einsum('bl,valce->vabce', deriv, normal_flux(metric[1], state), precision=HIGHEST)
    volume = volume + jnp.einsum('cl,vable->vabce', deriv, normal_flux(metric[2], state), precision=HIGHEST)
    pieces = []
    for face in range(6):
        rows = face_parts(metric[face // 2])[face]
        pieces.append(rows if face % 2 == 1 else -rows)
    normals = jnp.concatenate(pieces, axis=-1)
    table = jnp.concatenate([traces, before, after], axis=-1)
    links = neighbor.reshape(4, 6 * count)
    kinds = mortar.reshape(6 * count)[None, None, None, :]
    gathered = [table[..., links[slot_number]] for slot_number in range(4)]
    outer = jnp.where(kinds == 0, gathered[0], jnp.zeros_like(gathered[0]))
    for kind in range(1, 5):
        fine = apply_pair(interp[(kind - 1) // 2], interp[(kind - 1) % 2], gathered[0])
        outer = outer + jnp.where(kinds == kind, fine, jnp.zeros_like(fine))
    coarse = apply_pair(project[0], project[0], gathered[0])
    for quarter in range(1, 4):
        coarse = coarse + apply_pair(project[quarter // 2], project[quarter % 2], gathered[quarter])
    outer = outer + jnp.where(kinds == 5, coarse, jnp.zeros_like(coarse))
    inner_flux = normal_flux(normals, traces)
    outer_flux = normal_flux(normals, outer)
    speed = speed_bound * (jnp.abs(normals[0]) + jnp.abs(normals[1]) + jnp.abs(normals[2]))
    upwind = 0.5 * (inner_flux + outer_flux) - 0.5 * speed * (outer - traces)
    lift = (upwind - inner_flux) * lift_scale
    volume = volume.at[:, 0].add(lift[..., 0:count])
    volume = volume.at[:, -1].add(lift[..., count:2 * count])
    volume = volume.at[:, :, 0].add(lift[..., 2 * count:3 * count])
    volume = volume.at[:, :, -1].add(lift[..., 3 * count:4 * count])
    volume = volume.at[:, :, :, 0].add(lift[..., 4 * count:5 * count])
    volume = volume.at[:, :, :, -1].add(lift[..., 5 * count:6 * count])
    return -inv_jac * volume


def per_rank(array):
    shaped = array.reshape(array.shape[:-1] + (RANKS, array.shape[-1] // RANKS))
    return jnp.moveaxis(shaped, -2, 0)


def placement(owners):
    position = jnp.arange(ELEM_DEV, dtype=jnp.int32)
    same = owners[:, :, None] == owners[:, None, :]
    earlier = position[None, None, :] < position[None, :, None]
    slot = jnp.sum((same & earlier).astype(jnp.int32), axis=-1)
    sources = jnp.arange(RANKS, dtype=jnp.int32)[:, None]
    delta = owners - sources
    kept = 2 * CAP + position[None, :]
    upper = (2 - delta) * CAP + slot
    lower = 2 * CAP + ELEM_DEV + (-delta - 1) * CAP + slot
    spot = jnp.where(delta == 0, kept, jnp.where(delta > 0, upper, lower))
    return (owners * PARENT_SLOTS + spot).reshape(-1).astype(jnp.int32)


def reference(coeffs, refine_flag, new_owner, inv_jac, metric, neighbor, mortar, export_up, export_down):
    tables = node_tables()
    owners = new_owner.reshape(RANKS, ELEM_DEV)
    target = placement(owners)
    parents = jnp.zeros(coeffs.shape[:-1] + (RANKS * PARENT_SLOTS,), jnp.float32).at[..., target].set(coeffs)
    refined = jnp.zeros((RANKS * PARENT_SLOTS,), jnp.int32).at[target].set(refine_flag)
    state = refine_elements(parents, refined > 0, tables[1])
    states = per_rank(state)

    def exported(inputs):
        state_rank, up_rows, down_rows = inputs
        traces = face_traces(state_rank)
        return traces[..., up_rows], traces[..., down_rows]

    sent_up, sent_down = lax.map(exported, (states, per_rank(export_up), per_rank(export_down)))
    before = jnp.concatenate([jnp.zeros_like(sent_up[:1]), sent_up[:-1]], axis=0)
    after = jnp.concatenate([sent_down[1:], jnp.zeros_like(sent_down[:1])], axis=0)

    def one_rank(inputs):
        state_rank, metric_rank, jac_rank, links, kinds, from_before, from_after = inputs
        traces = face_traces(state_rank)
        return right_side(state_rank, metric_rank, jac_rank, links, kinds, traces, from_before, from_after, tables)

    result = lax.map(one_rank, (states, per_rank(metric), per_rank(inv_jac), per_rank(neighbor),
                                per_rank(mortar), before, after))
    return jnp.moveaxis(result, 0, -2).reshape(state.shape)
```

```python
import functools

import jax
import jax.numpy as jnp
import ml_dtypes
import numpy as np
from jax import lax
from jax.experimental import pallas as pl
from jax.experimental.pallas import tpu as pltpu
from jax.sharding import PartitionSpec as P

ORDER = 4
NP = ORDER + 1
AXES = ("gx", "gy", "gz")
mean_flow = (0.5, 0.3, 0.2)
speed_bound = 1.5
band_steps = (2, 1, -1, -2)
F32 = jnp.float32
BF16 = jnp.bfloat16
MESH = pl.DeviceIdType.MESH


def lobatto_rule(degree):
    count = degree + 1
    nodes = np.cos(np.pi * np.arange(count) / degree)
    table = np.zeros((count, count))

    def fill():
        table[:, 0] = 1.0
        table[:, 1] = nodes
        for power in range(2, count):
            table[:, power] = (
                (2 * power - 1) * nodes * table[:, power - 1] - (power - 1) * table[:, power - 2]
            ) / power

    for sweep in range(80):
        fill()
        nodes = nodes - (nodes * table[:, degree] - table[:, degree - 1]) / (
            count * table[:, degree]
        )
    fill()
    weights = 2.0 / (degree * count * table[:, degree] ** 2)
    return (np.array(nodes[::-1]), np.array(weights[::-1]))


def node_tables():
    count = NP
    nodes, weights = lobatto_rule(ORDER)
    bary = np.array(
        [
            1.0 / np.prod([nodes[k] - nodes[other] for other in range(count) if other != k])
            for k in range(count)
        ]
    )
    deriv = np.zeros((count, count))
    for row in range(count):
        for column in range(count):
            if row != column:
                deriv[row, column] = bary[column] / bary[row] / (nodes[row] - nodes[column])
        deriv[row, row] = -np.sum(deriv[row])
    interp = np.zeros((2, count, count))
    for half in range(2):
        points = (nodes + 2.0 * half - 1.0) / 2.0
        for column in range(count):
            value = np.ones(count)
            for other in range(count):
                if other != column:
                    value = value * (points - nodes[other]) / (nodes[column] - nodes[other])
            interp[half, :, column] = value
    project = (
        0.5 * np.transpose(interp, (0, 2, 1)) * weights[None, None, :] / weights[None, :, None]
    )
    return deriv, interp, project, float(1.0 / weights[0])


def split_np(array):
    array = np.asarray(array, np.float32)
    high = array.astype(ml_dtypes.bfloat16)
    low = (array - high.astype(np.float32)).astype(ml_dtypes.bfloat16)
    return high, low


def widen(matrix, rows=True, columns=True):
    block = matrix.reshape(25, 5, 25, 5)
    full = np.zeros((25, 8, 25, 8))
    full[:, :5, :, :5] = block
    return full.reshape(200, 200)


def operators():
    deriv, interp, project, lift_scale = node_tables()
    eye = np.eye(NP)
    kron3 = lambda x, y, z: np.kron(np.kron(x, y), z)
    refine = np.zeros((256, 8 * 256))
    for child in range(8):
        h = (child // 4, child // 2 % 2, child % 2)
        whole = widen(kron3(interp[h[0]], interp[h[1]], interp[h[2]]))
        refine[:200, child * 256 : child * 256 + 200] = whole.T
    slope = np.concatenate(
        [
            widen(kron3(deriv, eye, eye)),
            widen(kron3(eye, deriv, eye)),
            widen(kron3(eye, eye, deriv)),
        ],
        axis=1,
    )
    pick = np.zeros((6 * 32, 200))
    for face in range(6):
        for m1 in range(NP):
            for m2 in range(NP):
                end = ORDER * (face % 2)
                node = [(end, m1, m2), (m1, end, m2), (m1, m2, end)][face // 2]
                pick[face * 32 + m1 * NP + m2, (node[0] * 5 + node[1]) * 8 + node[2]] = 1.0
    pairs = [np.kron(eye, eye)]
    pairs += [np.kron(interp[k // 2], interp[k % 2]) for k in range(4)]
    pairs += [np.kron(project[k // 2], project[k % 2]) for k in range(4)]
    mortar = np.zeros((9 * 160, 128))
    for number, pair in enumerate(pairs):
        for v in range(5):
            top = number * 160 + v * 32
            mortar[top : top + 25, v * 25 : v * 25 + 25] = pair
    mortar_high, mortar_low = split_np(mortar)
    mortar_twice = np.concatenate([mortar_high, mortar_high], axis=1)
    spread = lambda x: x.astype(ml_dtypes.bfloat16)
    arrays = (
        *split_np(refine),
        *split_np(slope),
        spread(pick),
        spread(pick.T.copy()),
        mortar_twice,
        mortar_low,
    )
    return arrays, lift_scale


def split(value):
    high = value.astype(BF16)
    return high, (value - high.astype(F32)).astype(BF16)


def dot(left, right):
    return jnp.dot(left, right, preferred_element_type=F32)


def one_hot(index, chunks):
    count = index.shape[1]
    rows = lax.broadcasted_iota(jnp.int32, (256, count), 0)
    parts = []
    for chunk in range(chunks):
        parts.append(
            jnp.where(rows == index - chunk * 256, 1.0, 0.0).astype(BF16)
        )
    return jnp.concatenate(parts, axis=0)


def body(
    sizes,
    lift_scale,
    coeffs_ref,
    flag_ref,
    owner_ref,
    jac_ref,
    metric_ref,
    near_ref,
    kind_ref,
    up_ref,
    down_ref,
    refine_hi,
    refine_lo,
    slope_hi,
    slope_lo,
    pick,
    pick_t,
    mortar_hi,
    mortar_lo,
    out_ref,
    packed,
    leaving,
    arriving,
    state,
    rows_of,
    flux_hi,
    flux_lo,
    volume,
    inner,
    normal,
    flat,
    table,
    sending,
    halo,
    lift,
    send_sem,
    recv_sem,
):
    nx, ny, nz = sizes
    total = nx * ny * nz
    rank = (lax.axis_index("gx") * ny + lax.axis_index("gy")) * nz + lax.axis_index("gz")

    def place(steps):
        other = lax.rem(rank + steps + total, total)
        return (other // (ny * nz), lax.rem(other // nz, ny), lax.rem(other, nz))

    barrier = pltpu.get_barrier_semaphore()
    for steps in band_steps:
        pl.semaphore_signal(barrier, inc=1, device_id=place(steps), device_id_type=MESH)

    count = coeffs_ref.shape[-1]
    packed[...] = jnp.zeros_like(packed)
    for block in range(125):
        v, ab = divmod(block, 25)
        packed[pl.ds(v * 256 + ab * 8, 5), :] = coeffs_ref[block]
    owner = jnp.broadcast_to(owner_ref[...], (count, count))
    first = lax.broadcasted_iota(jnp.int32, (count, count), 0)
    second = lax.broadcasted_iota(jnp.int32, (count, count), 1)
    column = jnp.sum(jnp.where(first == second, owner, 0), axis=1, keepdims=True)
    slot = jnp.sum(
        jnp.where((column == owner) & (first < second), 1, 0), axis=0, keepdims=True
    )
    delta = owner_ref[...] - rank
    band = jnp.where(delta > 0, 2 - delta, 1 - delta)
    own_place = 32 + lax.broadcasted_iota(jnp.int32, (1, count), 1)
    spot = jnp.where(delta == 0, own_place, band * 8 + slot)
    slots = 32 + count
    chosen = jnp.where(
        lax.broadcasted_iota(jnp.int32, (slots, count), 0) == spot, 1.0, 0.0
    ).astype(F32)
    placed = lax.dot_general(
        chosen,
        packed[...],
        (((1,), (1,)), ((), ())),
        precision=lax.Precision.HIGHEST,
        preferred_element_type=F32,
    )
    flags = jnp.sum(chosen * flag_ref[...].astype(F32), axis=1, keepdims=True)
    flags = jnp.broadcast_to(flags, (slots, 128))
    for k in range(4):
        leaving[k, :, 0:1280] = placed[k * 8 : k * 8 + 8]
        leaving[k, :, 1280:1408] = flags[k * 8 : k * 8 + 8]

    pl.semaphore_wait(barrier, 4)
    moves = []
    for k in range(4):
        move = pltpu.make_async_remote_copy(
            src_ref=leaving.at[k],
            dst_ref=arriving.at[k],
            send_sem=send_sem.at[k],
            recv_sem=recv_sem.at[k],
            device_id=place(band_steps[k]),
            device_id_type=MESH,
        )
        move.start()
        moves.append(move)

    rows_of[...] = jnp.zeros_like(rows_of)
    for i in range(3):
        for j in range(3):
            rows_of[i, :, 0:5, j * 256 : j * 256 + 256] = metric_ref[
                i * 25 : i * 25 + 25, :, j, :
            ]
    for i in range(3):
        high, low = split(rows_of[i].reshape(200, 768))
        faces = pick[i * 64 : i * 64 + 64, :]
        normal[i * 64 : i * 64 + 64, :] = dot(faces, high) + dot(faces, low)
    for move in moves:
        move.wait()

    parents = [
        jnp.concatenate(
            [arriving[k, :, v * 256 : v * 256 + 256] for k in range(4)]
            + [placed[32:, v * 256 : v * 256 + 256]],
            axis=0,
        )
        for v in range(5)
    ]
    high, low = split(jnp.concatenate(parents, axis=0))
    spread = dot(high, refine_hi[...]) + dot(low, refine_hi[...]) + dot(high, refine_lo[...])
    refined = jnp.concatenate([arriving[k, :, 1280:1281] for k in range(4)] + [flags[32:, 0:1]], axis=0)
    row = lax.broadcasted_iota(jnp.int32, (slots, 256), 0)
    lane = lax.broadcasted_iota(jnp.int32, (slots, 256), 1)
    number, within = row >> 3, row & 7
    width = count // 4
    far = jnp.where(number < 2, number * width, count + number * width) + within
    far = jnp.where(within < width, far, -1000)
    base = 8 * jnp.where(row >= 32, 2 * width + row - 32, far)
    routes = [jnp.where(lane == base + child, refined, 0.0) for child in range(8)]
    routes.append(jnp.where(lane == base, 1.0 - refined, 0.0))
    route = jnp.concatenate(routes, axis=0).astype(BF16)
    over = (((0,), (0,)), ((), ()))
    for v in range(5):
        pieces = [spread[v * slots : (v + 1) * slots, c * 256 : c * 256 + 256] for c in range(8)]
        stacked = jnp.concatenate(pieces + [parents[v]], axis=0)
        high, low = split(stacked)
        value = lax.dot_general(high, route, over, preferred_element_type=F32)
        value = value + lax.dot_general(low, route, over, preferred_element_type=F32)
        state[:, v * 256 : v * 256 + 256] = value[0:200]

    high, low = split(state[...])
    inner[...] = dot(pick[...], high) + dot(pick[...], low)
    flat[...] = jnp.zeros_like(flat)
    for f in range(6):
        for v in range(5):
            flat[v * 25 : v * 25 + 25, f * 256 : f * 256 + 256] = inner[
                f * 32 : f * 32 + 25, v * 256 : v * 256 + 256
            ]
    high, low = split(flat[...])
    table[0:128, 0:1536] = high
    table[128:256, 0:1536] = low
    copies = []
    for k, (index_ref, steps) in enumerate(((up_ref, 1), (down_ref, -1))):
        got = dot(table[:, 0:1536], one_hot(index_ref[...], 6))
        sending[k] = got[0:128] + got[128:256]
        copy = pltpu.make_async_remote_copy(
            src_ref=sending.at[k],
            dst_ref=halo.at[k],
            send_sem=send_sem.at[4 + k],
            recv_sem=recv_sem.at[4 + k],
            device_id=place(steps),
            device_id_type=MESH,
        )
        copy.start()
        copies.append(copy)

    values = [state[:, v * 256 : v * 256 + 256] for v in range(5)]
    for i in range(3):
        n = [rows_of[i, :, :, j * 256 : j * 256 + 256].reshape(200, 256) for j in range(3)]
        along = n[0] * values[1] + n[1] * values[2] + n[2] * values[3]
        carried = mean_flow[0] * n[0] + mean_flow[1] * n[1] + mean_flow[2] * n[2]
        parts = [carried * values[0] + along]
        parts += [carried * values[1 + j] + n[j] * values[4] for j in range(3)]
        parts.append(carried * values[4] + along)
        for v in range(5):
            high, low = split(parts[v])
            flux_hi[i, :, v * 256 : v * 256 + 256] = high
            flux_lo[i, :, v * 256 : v * 256 + 256] = low
    gathered = None
    for i in range(3):
        cut = slice(i * 200, i * 200 + 200)
        term = (
            dot(slope_hi[:, cut], flux_hi[i])
            + dot(slope_hi[:, cut], flux_lo[i])
            + dot(slope_lo[:, cut], flux_hi[i])
        )
        gathered = term if gathered is None else gathered + term
    volume[...] = gathered

    for k, copy in enumerate(copies):
        copy.wait()
        real = rank > 0 if k == 0 else rank < total - 1
        high, low = split(jnp.where(real, halo[k], 0.0))
        table[0:128, 1536 + k * 256 : 1792 + k * 256] = high
        table[128:256, 1536 + k * 256 : 1792 + k * 256] = low

    def one_face(f, carry):
        links = near_ref[f]
        kind = kind_ref[pl.ds(f, 1), :]
        g = [
            dot(table[...], one_hot(links[q : q + 1, :], 8)).astype(BF16) for q in range(4)
        ]
        fine = dot(mortar_hi[0:960, :], g[0]) + dot(mortar_lo[0:960, :], g[0][0:128])
        coarse = fine[800:960]
        for q in range(1, 4):
            cut = slice(800 + q * 160, 960 + q * 160)
            coarse = coarse + dot(mortar_hi[cut, :], g[q]) + dot(mortar_lo[cut, :], g[q][0:128])
        outer = jnp.where(kind == 5, coarse, fine[0:160])
        for k in range(1, 5):
            outer = jnp.where(kind == k, fine[k * 160 : k * 160 + 160], outer)
        top = pl.multiple_of(f * 32, 32)
        side = jnp.where(lax.rem(f, 2) == 1, 1.0, -1.0)
        n = [normal[pl.ds(top, 32), j * 256 : j * 256 + 256] * side for j in range(3)]
        d = [
            outer[v * 32 : v * 32 + 32] - inner[pl.ds(top, 32), v * 256 : v * 256 + 256]
            for v in range(5)
        ]
        speed = speed_bound * (jnp.abs(n[0]) + jnp.abs(n[1]) + jnp.abs(n[2]))
        along = n[0] * d[1] + n[1] * d[2] + n[2] * d[3]
        excess = mean_flow[0] * n[0] + mean_flow[1] * n[1] + mean_flow[2] * n[2] - speed
        parts = [excess * d[0] + along]
        parts += [excess * d[1 + j] + n[j] * d[4] for j in range(3)]
        parts.append(excess * d[4] + along)
        for v in range(5):
            lift[pl.ds(top, 32), v * 256 : v * 256 + 256] = (0.5 * lift_scale) * parts[v]
        return carry

    lax.fori_loop(0, 6, one_face, 0)

    high, low = split(lift[...])
    result = volume[...] + dot(pick_t[...], high) + dot(pick_t[...], low)
    for v in range(5):
        piece = result[:, v * 256 : v * 256 + 256].reshape(25, 8, 256)[:, 0:5, :]
        out_ref[v * 25 : v * 25 + 25] = -jac_ref[...] * piece


def local(
    sizes, coeffs, refine_flag, new_owner, inv_jac, metric, neighbor, mortar, export_up, export_down
):
    constants, lift_scale = operators()
    count = coeffs.shape[-1]
    elements = inv_jac.shape[-1]
    operands = (
        coeffs.reshape(125, 5, count),
        refine_flag.reshape(1, count),
        new_owner.reshape(1, count),
        inv_jac.reshape(25, 5, elements),
        jnp.transpose(metric, (0, 2, 3, 4, 1, 5)).reshape(75, 5, 3, elements),
        jnp.transpose(neighbor, (1, 0, 2)),
        mortar,
        export_up.reshape(1, elements),
        export_down.reshape(1, elements),
    ) + tuple(jnp.asarray(c) for c in constants)
    vmem = pl.BlockSpec(memory_space=pltpu.VMEM)
    out = pl.pallas_call(
        functools.partial(body, sizes, lift_scale),
        out_shape=jax.ShapeDtypeStruct((125, 5, elements), F32),
        in_specs=[vmem] * len(operands),
        out_specs=vmem,
        scratch_shapes=[
            pltpu.VMEM((1280, count), F32),
            pltpu.VMEM((4, 8, 1408), F32),
            pltpu.VMEM((4, 8, 1408), F32),
            pltpu.VMEM((200, 1280), F32),
            pltpu.VMEM((3, 25, 8, 768), F32),
            pltpu.VMEM((3, 200, 1280), BF16),
            pltpu.VMEM((3, 200, 1280), BF16),
            pltpu.VMEM((200, 1280), F32),
            pltpu.VMEM((192, 1280), F32),
            pltpu.VMEM((192, 768), F32),
            pltpu.VMEM((128, 1536), F32),
            pltpu.VMEM((256, 2048), BF16),
            pltpu.VMEM((2, 128, 256), F32),
            pltpu.VMEM((2, 128, 256), F32),
            pltpu.VMEM((192, 1280), F32),
            pltpu.SemaphoreType.DMA((6,)),
            pltpu.SemaphoreType.DMA((6,)),
        ],
        compiler_params=pltpu.CompilerParams(
            collective_id=0, has_side_effects=True, vmem_limit_bytes=56 * 2**20
        ),
    )(*operands)
    return out.reshape(5, 5, 5, 5, elements)


def solution(mesh):
    sizes = tuple(mesh.shape[axis] for axis in AXES)
    in_specs = (
        P(None, None, None, None, AXES),
        P(AXES),
        P(AXES),
        P(None, None, None, AXES),
        P(None, None, None, None, None, AXES),
        P(None, None, AXES),
        P(None, AXES),
        P(AXES),
        P(AXES),
    )
    return jax.shard_map(
        functools.partial(local, sizes),
        mesh=mesh,
        in_specs=in_specs,
        out_specs=P(None, None, None, None, AXES),
        check_vma=False,
    )
```

```python
import functools

import jax
import jax.numpy as jnp
import ml_dtypes
import numpy as np
from jax import lax
from jax.experimental import pallas as pl
from jax.experimental.pallas import tpu as pltpu
from jax.sharding import PartitionSpec as P

ORDER = 4
NP = ORDER + 1
AXES = ("gx", "gy", "gz")
mean_flow = (0.5, 0.3, 0.2)
speed_bound = 1.5
band_steps = (2, 1, -1, -2)
F32 = jnp.float32
BF16 = jnp.bfloat16
MESH = pl.DeviceIdType.MESH


def lobatto_rule(degree):
    count = degree + 1
    nodes = np.cos(np.pi * np.arange(count) / degree)
    table = np.zeros((count, count))

    def fill():
        table[:, 0] = 1.0
        table[:, 1] = nodes
        for power in range(2, count):
            table[:, power] = (
                (2 * power - 1) * nodes * table[:, power - 1] - (power - 1) * table[:, power - 2]
            ) / power

    for sweep in range(80):
        fill()
        nodes = nodes - (nodes * table[:, degree] - table[:, degree - 1]) / (
            count * table[:, degree]
        )
    fill()
    weights = 2.0 / (degree * count * table[:, degree] ** 2)
    return (np.array(nodes[::-1]), np.array(weights[::-1]))


def node_tables():
    count = NP
    nodes, weights = lobatto_rule(ORDER)
    bary = np.array(
        [
            1.0 / np.prod([nodes[k] - nodes[other] for other in range(count) if other != k])
            for k in range(count)
        ]
    )
    deriv = np.zeros((count, count))
    for row in range(count):
        for column in range(count):
            if row != column:
                deriv[row, column] = bary[column] / bary[row] / (nodes[row] - nodes[column])
        deriv[row, row] = -np.sum(deriv[row])
    interp = np.zeros((2, count, count))
    for half in range(2):
        points = (nodes + 2.0 * half - 1.0) / 2.0
        for column in range(count):
            value = np.ones(count)
            for other in range(count):
                if other != column:
                    value = value * (points - nodes[other]) / (nodes[column] - nodes[other])
            interp[half, :, column] = value
    project = (
        0.5 * np.transpose(interp, (0, 2, 1)) * weights[None, None, :] / weights[None, :, None]
    )
    return deriv, interp, project, float(1.0 / weights[0])


def split_np(array):
    array = np.asarray(array, np.float32)
    high = array.astype(ml_dtypes.bfloat16)
    low = (array - high.astype(np.float32)).astype(ml_dtypes.bfloat16)
    return high, low


def widen(matrix, rows=True, columns=True):
    block = matrix.reshape(25, 5, 25, 5)
    full = np.zeros((25, 8, 25, 8))
    full[:, :5, :, :5] = block
    return full.reshape(200, 200)


def operators():
    deriv, interp, project, lift_scale = node_tables()
    eye = np.eye(NP)
    kron3 = lambda x, y, z: np.kron(np.kron(x, y), z)
    refine = np.zeros((256, 8 * 256))
    for child in range(8):
        h = (child // 4, child // 2 % 2, child % 2)
        whole = widen(kron3(interp[h[0]], interp[h[1]], interp[h[2]]))
        refine[:200, child * 256 : child * 256 + 200] = whole.T
    slope = np.concatenate(
        [
            widen(kron3(deriv, eye, eye)),
            widen(kron3(eye, deriv, eye)),
            widen(kron3(eye, eye, deriv)),
        ],
        axis=1,
    )
    pick = np.zeros((6 * 32, 200))
    for face in range(6):
        for m1 in range(NP):
            for m2 in range(NP):
                end = ORDER * (face % 2)
                node = [(end, m1, m2), (m1, end, m2), (m1, m2, end)][face // 2]
                pick[face * 32 + m1 * NP + m2, (node[0] * 5 + node[1]) * 8 + node[2]] = 1.0
    pairs = [np.kron(eye, eye)]
    pairs += [np.kron(interp[k // 2], interp[k % 2]) for k in range(4)]
    pairs += [np.kron(project[k // 2], project[k % 2]) for k in range(4)]
    mortar = np.zeros((9 * 160, 128))
    for number, pair in enumerate(pairs):
        for v in range(5):
            top = number * 160 + v * 32
            mortar[top : top + 25, v * 25 : v * 25 + 25] = pair
    mortar_high, mortar_low = split_np(mortar)
    mortar_twice = np.concatenate([mortar_high, mortar_high], axis=1)
    spread = lambda x: x.astype(ml_dtypes.bfloat16)
    arrays = (
        *split_np(refine),
        *split_np(slope),
        spread(pick),
        spread(pick.T.copy()),
        mortar_twice,
        mortar_low,
    )
    return arrays, lift_scale


def split(value):
    high = value.astype(BF16)
    return high, (value - high.astype(F32)).astype(BF16)


def dot(left, right):
    return jnp.dot(left, right, preferred_element_type=F32)


def one_hot(index, chunks):
    count = index.shape[1]
    rows = lax.broadcasted_iota(jnp.int32, (256, count), 0).astype(F32).astype(BF16)
    part, low = index >> 8, (index & 255).astype(F32)
    one, zero = jnp.ones((), BF16), jnp.zeros((), BF16)
    parts = []
    for chunk in range(chunks):
        here = jnp.where(part == chunk, low, -1.0).astype(BF16)
        parts.append(jnp.where(rows == here, one, zero))
    return jnp.concatenate(parts, axis=0)


def body(
    sizes,
    lift_scale,
    coeffs_ref,
    flag_ref,
    owner_ref,
    near_ref,
    kind_ref,
    up_ref,
    down_ref,
    pick,
    *rest,
):
    late, out_ref, late_here = rest[0:9], rest[9], rest[10:19]
    (
        packed,
        leaving,
        arriving,
        state,
        rows_of,
        flux_hi,
        flux_lo,
        volume,
        inner,
        normal,
        flat,
        table,
        sending,
        halo,
        lift,
        send_sem,
        recv_sem,
        load_sem,
    ) = rest[19:]
    nx, ny, nz = sizes
    total = nx * ny * nz
    rank = (lax.axis_index("gx") * ny + lax.axis_index("gy")) * nz + lax.axis_index("gz")

    def place(steps):
        other = lax.rem(rank + steps + total, total)
        return (other // (ny * nz), lax.rem(other // nz, ny), lax.rem(other, nz))

    def there(steps):
        return (rank + steps >= 0) & (rank + steps < total)

    barrier = pltpu.get_barrier_semaphore()
    for steps in band_steps:

        @pl.when(there(steps))
        def _(steps=steps):
            pl.semaphore_signal(barrier, inc=1, device_id=place(steps), device_id_type=MESH)

    loads = []
    for number, (source, target) in enumerate(zip(late, late_here)):
        load = pltpu.make_async_copy(source, target, load_sem.at[number])
        load.start()
        loads.append(load)
    metric_ref, refine_hi, refine_lo, slope_hi, slope_lo, pick_t, mortar_hi, mortar_lo, jac_ref = late_here

    count = coeffs_ref.shape[-1]
    packed[...] = jnp.zeros_like(packed)
    for block in range(125):
        v, ab = divmod(block, 25)
        packed[pl.ds(v * 256 + ab * 8, 5), :] = coeffs_ref[block]
    owner = jnp.broadcast_to(owner_ref[...], (count, count))
    first = lax.broadcasted_iota(jnp.int32, (count, count), 0)
    second = lax.broadcasted_iota(jnp.int32, (count, count), 1)
    column = jnp.sum(jnp.where(first == second, owner, 0), axis=1, keepdims=True)
    slot = jnp.sum(
        jnp.where((column == owner) & (first < second), 1, 0), axis=0, keepdims=True
    )
    delta = owner_ref[...] - rank
    band = jnp.where(delta > 0, 2 - delta, 1 - delta)
    own_place = 32 + lax.broadcasted_iota(jnp.int32, (1, count), 1)
    spot = jnp.where(delta == 0, own_place, band * 8 + slot)
    slots = 32 + count
    chosen = jnp.where(
        lax.broadcasted_iota(jnp.int32, (slots, count), 0) == spot, 1.0, 0.0
    ).astype(F32)
    placed = lax.dot_general(
        chosen,
        packed[...],
        (((1,), (1,)), ((), ())),
        precision=lax.Precision.HIGHEST,
        preferred_element_type=F32,
    )
    flags = jnp.sum(chosen * flag_ref[...].astype(F32), axis=1, keepdims=True)
    flags = jnp.broadcast_to(flags, (slots, 128))
    for k in range(4):
        leaving[k, :, 0:1280] = placed[k * 8 : k * 8 + 8]
        leaving[k, :, 1280:1408] = flags[k * 8 : k * 8 + 8]

    around = sum(there(steps).astype(jnp.int32) for steps in band_steps)
    pl.semaphore_wait(barrier, around)
    moves = []
    for k in range(4):
        move = pltpu.make_async_remote_copy(
            src_ref=leaving.at[k],
            dst_ref=arriving.at[k],
            send_sem=send_sem.at[k],
            recv_sem=recv_sem.at[k],
            device_id=place(band_steps[k]),
            device_id_type=MESH,
        )
        pl.when(there(band_steps[k]))(move.start)
        moves.append(move)

        @pl.when(jnp.logical_not(there(-band_steps[k])))
        def _(k=k):
            arriving[k] = jnp.zeros_like(arriving[k])

    loads[0].wait()

    rows_of[...] = jnp.zeros_like(rows_of)
    for i in range(3):
        for j in range(3):
            rows_of[i, :, 0:5, j * 256 : j * 256 + 256] = metric_ref[
                i * 25 : i * 25 + 25, :, j, :
            ]
    for i in range(3):
        high, low = split(rows_of[i].reshape(200, 768))
        faces = pick[i * 64 : i * 64 + 64, :]
        normal[i * 64 : i * 64 + 64, :] = dot(faces, high) + dot(faces, low)
    loads[1].wait()
    loads[2].wait()
    for k, move in enumerate(moves):
        pl.when(there(-band_steps[k]))(move.wait_recv)

    parents = [
        jnp.concatenate(
            [arriving[k, :, v * 256 : v * 256 + 256] for k in range(4)]
            + [placed[32:, v * 256 : v * 256 + 256]],
            axis=0,
        )
        for v in range(5)
    ]
    high, low = split(jnp.concatenate(parents, axis=0))
    spread = dot(high, refine_hi[...]) + dot(low, refine_hi[...]) + dot(high, refine_lo[...])
    refined = jnp.concatenate([arriving[k, :, 1280:1281] for k in range(4)] + [flags[32:, 0:1]], axis=0)
    row = lax.broadcasted_iota(jnp.int32, (slots, 256), 0)
    lane = lax.broadcasted_iota(jnp.int32, (slots, 256), 1)
    number, within = row >> 3, row & 7
    width = count // 4
    far = jnp.where(number < 2, number * width, count + number * width) + within
    far = jnp.where(within < width, far, -1000)
    base = 8 * jnp.where(row >= 32, 2 * width + row - 32, far)
    routes = [jnp.where(lane == base + child, refined, 0.0) for child in range(8)]
    routes.append(jnp.where(lane == base, 1.0 - refined, 0.0))
    route = jnp.concatenate(routes, axis=0).astype(BF16)
    over = (((0,), (0,)), ((), ()))
    for v in range(5):
        pieces = [spread[v * slots : (v + 1) * slots, c * 256 : c * 256 + 256] for c in range(8)]
        stacked = jnp.concatenate(pieces + [parents[v]], axis=0)
        high, low = split(stacked)
        value = lax.dot_general(high, route, over, preferred_element_type=F32)
        value = value + lax.dot_general(low, route, over, preferred_element_type=F32)
        state[:, v * 256 : v * 256 + 256] = value[0:200]

    high, low = split(state[...])
    inner[...] = dot(pick[...], high) + dot(pick[...], low)
    flat[...] = jnp.zeros_like(flat)
    for f in range(6):
        for v in range(5):
            flat[v * 25 : v * 25 + 25, f * 256 : f * 256 + 256] = inner[
                f * 32 : f * 32 + 25, v * 256 : v * 256 + 256
            ]
    high, low = split(flat[...])
    table[0:128, 0:1536] = high
    table[128:256, 0:1536] = low
    copies = []
    for k, (index_ref, steps) in enumerate(((up_ref, 1), (down_ref, -1))):
        got = dot(table[:, 0:1536], one_hot(index_ref[...], 6))
        sending[k] = got[0:128] + got[128:256]
        copy = pltpu.make_async_remote_copy(
            src_ref=sending.at[k],
            dst_ref=halo.at[k],
            send_sem=send_sem.at[4 + k],
            recv_sem=recv_sem.at[4 + k],
            device_id=place(steps),
            device_id_type=MESH,
        )
        pl.when(there(steps))(copy.start)
        copies.append((copy, steps))

        @pl.when(jnp.logical_not(there(-steps)))
        def _(k=k):
            halo[k] = jnp.zeros_like(halo[k])

    loads[3].wait()
    loads[4].wait()

    values = [state[:, v * 256 : v * 256 + 256] for v in range(5)]
    for i in range(3):
        n = [rows_of[i, :, :, j * 256 : j * 256 + 256].reshape(200, 256) for j in range(3)]
        along = n[0] * values[1] + n[1] * values[2] + n[2] * values[3]
        carried = mean_flow[0] * n[0] + mean_flow[1] * n[1] + mean_flow[2] * n[2]
        parts = [carried * values[0] + along]
        parts += [carried * values[1 + j] + n[j] * values[4] for j in range(3)]
        parts.append(carried * values[4] + along)
        for v in range(5):
            high, low = split(parts[v])
            flux_hi[i, :, v * 256 : v * 256 + 256] = high
            flux_lo[i, :, v * 256 : v * 256 + 256] = low
    gathered = None
    for i in range(3):
        cut = slice(i * 200, i * 200 + 200)
        term = (
            dot(slope_hi[:, cut], flux_hi[i])
            + dot(slope_hi[:, cut], flux_lo[i])
            + dot(slope_lo[:, cut], flux_hi[i])
        )
        gathered = term if gathered is None else gathered + term
    volume[...] = gathered

    for k, (copy, steps) in enumerate(copies):
        pl.when(there(-steps))(copy.wait_recv)
        high, low = split(halo[k])
        table[0:128, 1536 + k * 256 : 1792 + k * 256] = high
        table[128:256, 1536 + k * 256 : 1792 + k * 256] = low

    for load in loads[5:]:
        load.wait()

    def one_face(f, carry):
        links = near_ref[f]
        kind = kind_ref[pl.ds(f, 1), :]
        g = [
            dot(table[...], one_hot(links[q : q + 1, :], 8)).astype(BF16) for q in range(4)
        ]
        fine = dot(mortar_hi[0:960, :], g[0]) + dot(mortar_lo[0:960, :], g[0][0:128])
        coarse = fine[800:960]
        for q in range(1, 4):
            cut = slice(800 + q * 160, 960 + q * 160)
            coarse = coarse + dot(mortar_hi[cut, :], g[q]) + dot(mortar_lo[cut, :], g[q][0:128])
        outer = jnp.where(kind == 5, coarse, fine[0:160])
        for k in range(1, 5):
            outer = jnp.where(kind == k, fine[k * 160 : k * 160 + 160], outer)
        top = pl.multiple_of(f * 32, 32)
        side = jnp.where(lax.rem(f, 2) == 1, 1.0, -1.0)
        n = [normal[pl.ds(top, 32), j * 256 : j * 256 + 256] * side for j in range(3)]
        d = [
            outer[v * 32 : v * 32 + 32] - inner[pl.ds(top, 32), v * 256 : v * 256 + 256]
            for v in range(5)
        ]
        speed = speed_bound * (jnp.abs(n[0]) + jnp.abs(n[1]) + jnp.abs(n[2]))
        along = n[0] * d[1] + n[1] * d[2] + n[2] * d[3]
        excess = mean_flow[0] * n[0] + mean_flow[1] * n[1] + mean_flow[2] * n[2] - speed
        parts = [excess * d[0] + along]
        parts += [excess * d[1 + j] + n[j] * d[4] for j in range(3)]
        parts.append(excess * d[4] + along)
        for v in range(5):
            lift[pl.ds(top, 32), v * 256 : v * 256 + 256] = (0.5 * lift_scale) * parts[v]
        return carry

    lax.fori_loop(0, 6, one_face, 0)

    for k, move in enumerate(moves):
        pl.when(there(band_steps[k]))(move.wait_send)
    for copy, steps in copies:
        pl.when(there(steps))(copy.wait_send)
    high, low = split(lift[...])
    result = volume[...] + dot(pick_t[...], high) + dot(pick_t[...], low)
    for v in range(5):
        piece = result[:, v * 256 : v * 256 + 256].reshape(25, 8, 256)[:, 0:5, :]
        out_ref[v * 25 : v * 25 + 25] = -jac_ref[...] * piece


def local(
    sizes, coeffs, refine_flag, new_owner, inv_jac, metric, neighbor, mortar, export_up, export_down
):
    constants, lift_scale = operators()
    count = coeffs.shape[-1]
    elements = inv_jac.shape[-1]
    refine_hi, refine_lo, slope_hi, slope_lo, pick, pick_t, mortar_hi, mortar_lo = (
        jnp.asarray(c) for c in constants
    )
    rows = jnp.transpose(metric, (0, 2, 3, 4, 1, 5)).reshape(75, 5, 3, elements)
    jac = inv_jac.reshape(25, 5, elements)
    early = (
        coeffs.reshape(125, 5, count),
        refine_flag.reshape(1, count),
        new_owner.reshape(1, count),
        jnp.transpose(neighbor, (1, 0, 2)),
        mortar,
        export_up.reshape(1, elements),
        export_down.reshape(1, elements),
        pick,
    )
    late = (rows, refine_hi, refine_lo, slope_hi, slope_lo, pick_t, mortar_hi, mortar_lo, jac)
    vmem = pl.BlockSpec(memory_space=pltpu.VMEM)
    out = pl.pallas_call(
        functools.partial(body, sizes, lift_scale),
        out_shape=jax.ShapeDtypeStruct((125, 5, elements), F32),
        in_specs=[vmem] * len(early) + [pl.BlockSpec(memory_space=pl.ANY)] * len(late),
        out_specs=vmem,
        scratch_shapes=[pltpu.VMEM(x.shape, x.dtype) for x in late]
        + [
            pltpu.VMEM((1280, count), F32),
            pltpu.VMEM((4, 8, 1408), F32),
            pltpu.VMEM((4, 8, 1408), F32),
            pltpu.VMEM((200, 1280), F32),
            pltpu.VMEM((3, 25, 8, 768), F32),
            pltpu.VMEM((3, 200, 1280), BF16),
            pltpu.VMEM((3, 200, 1280), BF16),
            pltpu.VMEM((200, 1280), F32),
            pltpu.VMEM((192, 1280), F32),
            pltpu.VMEM((192, 768), F32),
            pltpu.VMEM((128, 1536), F32),
            pltpu.VMEM((256, 2048), BF16),
            pltpu.VMEM((2, 128, 256), F32),
            pltpu.VMEM((2, 128, 256), F32),
            pltpu.VMEM((192, 1280), F32),
            pltpu.SemaphoreType.DMA((6,)),
            pltpu.SemaphoreType.DMA((6,)),
            pltpu.SemaphoreType.DMA((9,)),
        ],
        compiler_params=pltpu.CompilerParams(
            collective_id=0, has_side_effects=True, vmem_limit_bytes=56 * 2**20
        ),
    )(*early, *late)
    return out.reshape(5, 5, 5, 5, elements)


def solution(mesh):
    sizes = tuple(mesh.shape[axis] for axis in AXES)
    in_specs = (
        P(None, None, None, None, AXES),
        P(AXES),
        P(AXES),
        P(None, None, None, AXES),
        P(None, None, None, None, None, AXES),
        P(None, None, AXES),
        P(None, AXES),
        P(AXES),
        P(AXES),
    )
    return jax.shard_map(
        functools.partial(local, sizes),
        mesh=mesh,
        in_specs=in_specs,
        out_specs=P(None, None, None, None, AXES),
        check_vma=False,
    )
```

```python
import functools

import jax
import jax.numpy as jnp
import ml_dtypes
import numpy as np
from jax import lax
from jax.experimental import pallas as pl
from jax.experimental.pallas import tpu as pltpu
from jax.sharding import PartitionSpec as P

ORDER = 4
NP = ORDER + 1
AXES = ("gx", "gy", "gz")
mean_flow = (0.5, 0.3, 0.2)
speed_bound = 1.5
band_steps = (2, 1, -1, -2)
F32 = jnp.float32
BF16 = jnp.bfloat16
MESH = pl.DeviceIdType.MESH


def lobatto_rule(degree):
    count = degree + 1
    nodes = np.cos(np.pi * np.arange(count) / degree)
    table = np.zeros((count, count))

    def fill():
        table[:, 0] = 1.0
        table[:, 1] = nodes
        for power in range(2, count):
            table[:, power] = (
                (2 * power - 1) * nodes * table[:, power - 1] - (power - 1) * table[:, power - 2]
            ) / power

    for sweep in range(80):
        fill()
        nodes = nodes - (nodes * table[:, degree] - table[:, degree - 1]) / (
            count * table[:, degree]
        )
    fill()
    weights = 2.0 / (degree * count * table[:, degree] ** 2)
    return (np.array(nodes[::-1]), np.array(weights[::-1]))


def node_tables():
    count = NP
    nodes, weights = lobatto_rule(ORDER)
    bary = np.array(
        [
            1.0 / np.prod([nodes[k] - nodes[other] for other in range(count) if other != k])
            for k in range(count)
        ]
    )
    deriv = np.zeros((count, count))
    for row in range(count):
        for column in range(count):
            if row != column:
                deriv[row, column] = bary[column] / bary[row] / (nodes[row] - nodes[column])
        deriv[row, row] = -np.sum(deriv[row])
    interp = np.zeros((2, count, count))
    for half in range(2):
        points = (nodes + 2.0 * half - 1.0) / 2.0
        for column in range(count):
            value = np.ones(count)
            for other in range(count):
                if other != column:
                    value = value * (points - nodes[other]) / (nodes[column] - nodes[other])
            interp[half, :, column] = value
    project = (
        0.5 * np.transpose(interp, (0, 2, 1)) * weights[None, None, :] / weights[None, :, None]
    )
    return deriv, interp, project, float(1.0 / weights[0])


def split_np(array):
    array = np.asarray(array, np.float32)
    high = array.astype(ml_dtypes.bfloat16)
    low = (array - high.astype(np.float32)).astype(ml_dtypes.bfloat16)
    return high, low


def widen(matrix, rows=True, columns=True):
    block = matrix.reshape(25, 5, 25, 5)
    full = np.zeros((25, 8, 25, 8))
    full[:, :5, :, :5] = block
    return full.reshape(200, 200)


def operators():
    deriv, interp, project, lift_scale = node_tables()
    eye = np.eye(NP)
    kron3 = lambda x, y, z: np.kron(np.kron(x, y), z)
    refine = np.zeros((256, 8 * 256))
    for child in range(8):
        h = (child // 4, child // 2 % 2, child % 2)
        whole = widen(kron3(interp[h[0]], interp[h[1]], interp[h[2]]))
        refine[:200, child * 256 : child * 256 + 200] = whole.T
    slope = np.concatenate(
        [
            widen(kron3(deriv, eye, eye)),
            widen(kron3(eye, deriv, eye)),
            widen(kron3(eye, eye, deriv)),
        ],
        axis=1,
    )
    pick = np.zeros((6 * 32, 200))
    for face in range(6):
        for m1 in range(NP):
            for m2 in range(NP):
                end = ORDER * (face % 2)
                node = [(end, m1, m2), (m1, end, m2), (m1, m2, end)][face // 2]
                pick[face * 32 + m1 * NP + m2, (node[0] * 5 + node[1]) * 8 + node[2]] = 1.0
    pairs = [np.kron(eye, eye)]
    pairs += [np.kron(interp[k // 2], interp[k % 2]) for k in range(4)]
    pairs += [np.kron(project[k // 2], project[k % 2]) for k in range(4)]
    mortar = np.zeros((9 * 160, 128))
    for number, pair in enumerate(pairs):
        for v in range(5):
            top = number * 160 + v * 32
            mortar[top : top + 25, v * 25 : v * 25 + 25] = pair
    mortar_high, mortar_low = split_np(mortar)
    mortar_twice = np.concatenate([mortar_high, mortar_high], axis=1)
    spread = lambda x: x.astype(ml_dtypes.bfloat16)
    arrays = (
        *split_np(refine),
        *split_np(slope),
        spread(pick),
        spread(pick.T.copy()),
        mortar_twice,
        mortar_low,
    )
    return arrays, lift_scale


def split(value):
    high = value.astype(BF16)
    return high, (value - high.astype(F32)).astype(BF16)


def dot(left, right):
    return jnp.dot(left, right, preferred_element_type=F32)


def one_hot(index, chunks):
    count = index.shape[1]
    rows = lax.broadcasted_iota(jnp.int32, (256, count), 0).astype(F32).astype(BF16)
    part, low = index >> 8, (index & 255).astype(F32)
    one, zero = jnp.ones((), BF16), jnp.zeros((), BF16)
    parts = []
    for chunk in range(chunks):
        here = jnp.where(part == chunk, low, -1.0).astype(BF16)
        parts.append(jnp.where(rows == here, one, zero))
    return jnp.concatenate(parts, axis=0)


def body(
    sizes,
    lift_scale,
    coeffs_ref,
    flag_ref,
    owner_ref,
    near_ref,
    kind_ref,
    up_ref,
    down_ref,
    pick,
    *rest,
):
    late, out_ref, late_here = rest[0:9], rest[9], rest[10:19]
    (
        packed,
        leaving,
        arriving,
        state,
        rows_of,
        flux_hi,
        flux_lo,
        volume,
        inner,
        normal,
        flat,
        table,
        sending,
        halo,
        lift,
        fetched,
        send_sem,
        recv_sem,
        load_sem,
    ) = rest[19:]
    nx, ny, nz = sizes
    total = nx * ny * nz
    rank = (lax.axis_index("gx") * ny + lax.axis_index("gy")) * nz + lax.axis_index("gz")

    def place(steps):
        other = lax.rem(rank + steps + total, total)
        return (other // (ny * nz), lax.rem(other // nz, ny), lax.rem(other, nz))

    def there(steps):
        return (rank + steps >= 0) & (rank + steps < total)

    barrier = pltpu.get_barrier_semaphore()
    for steps in band_steps:

        @pl.when(there(steps))
        def _(steps=steps):
            pl.semaphore_signal(barrier, inc=1, device_id=place(steps), device_id_type=MESH)

    loads = []
    for number, (source, target) in enumerate(zip(late, late_here)):
        load = pltpu.make_async_copy(source, target, load_sem.at[number])
        load.start()
        loads.append(load)
    metric_ref, refine_hi, refine_lo, slope_hi, slope_lo, pick_t, mortar_hi, mortar_lo, jac_ref = late_here

    count = coeffs_ref.shape[-1]
    packed[...] = jnp.zeros_like(packed)
    for block in range(125):
        v, ab = divmod(block, 25)
        packed[pl.ds(v * 256 + ab * 8, 5), :] = coeffs_ref[block]
    owner = jnp.broadcast_to(owner_ref[...], (count, count))
    first = lax.broadcasted_iota(jnp.int32, (count, count), 0)
    second = lax.broadcasted_iota(jnp.int32, (count, count), 1)
    column = jnp.sum(jnp.where(first == second, owner, 0), axis=1, keepdims=True)
    slot = jnp.sum(
        jnp.where((column == owner) & (first < second), 1, 0), axis=0, keepdims=True
    )
    delta = owner_ref[...] - rank
    band = jnp.where(delta > 0, 2 - delta, 1 - delta)
    own_place = 32 + lax.broadcasted_iota(jnp.int32, (1, count), 1)
    spot = jnp.where(delta == 0, own_place, band * 8 + slot)
    slots = 32 + count
    chosen = jnp.where(
        lax.broadcasted_iota(jnp.int32, (slots, count), 0) == spot, 1.0, 0.0
    ).astype(F32)
    along_lanes = (((1,), (1,)), ((), ()))
    high, low = split(packed[...])
    picked = chosen.astype(BF16)
    placed = lax.dot_general(picked, high, along_lanes, preferred_element_type=F32)
    placed = placed + lax.dot_general(picked, low, along_lanes, preferred_element_type=F32)
    flags = jnp.sum(chosen * flag_ref[...].astype(F32), axis=1, keepdims=True)
    flags = jnp.broadcast_to(flags, (slots, 128))
    for k in range(4):
        leaving[k, :, 0:1280] = placed[k * 8 : k * 8 + 8]
        leaving[k, :, 1280:1408] = flags[k * 8 : k * 8 + 8]

    around = sum(there(steps).astype(jnp.int32) for steps in band_steps)
    pl.semaphore_wait(barrier, around)
    moves = []
    for k in range(4):
        move = pltpu.make_async_remote_copy(
            src_ref=leaving.at[k],
            dst_ref=arriving.at[k],
            send_sem=send_sem.at[k],
            recv_sem=recv_sem.at[k],
            device_id=place(band_steps[k]),
            device_id_type=MESH,
        )
        pl.when(there(band_steps[k]))(move.start)
        moves.append(move)

        @pl.when(jnp.logical_not(there(-band_steps[k])))
        def _(k=k):
            arriving[k] = jnp.zeros_like(arriving[k])

    loads[0].wait()

    rows_of[...] = jnp.zeros_like(rows_of)
    for i in range(3):
        for j in range(3):
            rows_of[i, :, 0:5, j * 256 : j * 256 + 256] = metric_ref[
                i * 25 : i * 25 + 25, :, j, :
            ]
    for i in range(3):
        high, low = split(rows_of[i].reshape(200, 768))
        faces = pick[i * 64 : i * 64 + 64, :]
        normal[i * 64 : i * 64 + 64, :] = dot(faces, high) + dot(faces, low)
    loads[1].wait()
    loads[2].wait()
    for k, move in enumerate(moves):
        pl.when(there(-band_steps[k]))(move.wait_recv)

    parents = [
        jnp.concatenate(
            [arriving[k, :, v * 256 : v * 256 + 256] for k in range(4)]
            + [placed[32:, v * 256 : v * 256 + 256]],
            axis=0,
        )
        for v in range(5)
    ]
    high, low = split(jnp.concatenate(parents, axis=0))
    spread = dot(high, refine_hi[...]) + dot(low, refine_hi[...]) + dot(high, refine_lo[...])
    refined = jnp.concatenate([arriving[k, :, 1280:1281] for k in range(4)] + [flags[32:, 0:1]], axis=0)
    row = lax.broadcasted_iota(jnp.int32, (slots, 256), 0)
    lane = lax.broadcasted_iota(jnp.int32, (slots, 256), 1)
    number, within = row >> 3, row & 7
    width = count // 4
    far = jnp.where(number < 2, number * width, count + number * width) + within
    far = jnp.where(within < width, far, -1000)
    base = 8 * jnp.where(row >= 32, 2 * width + row - 32, far)
    routes = [jnp.where(lane == base + child, refined, 0.0) for child in range(8)]
    routes.append(jnp.where(lane == base, 1.0 - refined, 0.0))
    route = jnp.concatenate(routes, axis=0).astype(BF16)
    over = (((0,), (0,)), ((), ()))
    for v in range(5):
        pieces = [spread[v * slots : (v + 1) * slots, c * 256 : c * 256 + 256] for c in range(8)]
        stacked = jnp.concatenate(pieces + [parents[v]], axis=0)
        high, low = split(stacked)
        value = lax.dot_general(high, route, over, preferred_element_type=F32)
        value = value + lax.dot_general(low, route, over, preferred_element_type=F32)
        state[:, v * 256 : v * 256 + 256] = value[0:200]

    high, low = split(state[...])
    inner[...] = dot(pick[...], high) + dot(pick[...], low)
    flat[...] = jnp.zeros_like(flat)
    for f in range(6):
        for v in range(5):
            flat[v * 25 : v * 25 + 25, f * 256 : f * 256 + 256] = inner[
                f * 32 : f * 32 + 25, v * 256 : v * 256 + 256
            ]
    high, low = split(flat[...])
    table[0:128, 0:1536] = high
    table[128:256, 0:1536] = low
    copies = []
    for k, (index_ref, steps) in enumerate(((up_ref, 1), (down_ref, -1))):
        got = dot(table[:, 0:1536], one_hot(index_ref[...], 6))
        sending[k] = got[0:128] + got[128:256]
        copy = pltpu.make_async_remote_copy(
            src_ref=sending.at[k],
            dst_ref=halo.at[k],
            send_sem=send_sem.at[4 + k],
            recv_sem=recv_sem.at[4 + k],
            device_id=place(steps),
            device_id_type=MESH,
        )
        pl.when(there(steps))(copy.start)
        copies.append((copy, steps))

        @pl.when(jnp.logical_not(there(-steps)))
        def _(k=k):
            halo[k] = jnp.zeros_like(halo[k])

    loads[3].wait()
    loads[4].wait()

    values = [state[:, v * 256 : v * 256 + 256] for v in range(5)]
    for i in range(3):
        n = [rows_of[i, :, :, j * 256 : j * 256 + 256].reshape(200, 256) for j in range(3)]
        along = n[0] * values[1] + n[1] * values[2] + n[2] * values[3]
        carried = mean_flow[0] * n[0] + mean_flow[1] * n[1] + mean_flow[2] * n[2]
        parts = [carried * values[0] + along]
        parts += [carried * values[1 + j] + n[j] * values[4] for j in range(3)]
        parts.append(carried * values[4] + along)
        for v in range(5):
            high, low = split(parts[v])
            flux_hi[i, :, v * 256 : v * 256 + 256] = high
            flux_lo[i, :, v * 256 : v * 256 + 256] = low
    gathered = None
    for i in range(3):
        cut = slice(i * 200, i * 200 + 200)
        term = (
            dot(slope_hi[:, cut], flux_hi[i])
            + dot(slope_hi[:, cut], flux_lo[i])
            + dot(slope_lo[:, cut], flux_hi[i])
        )
        gathered = term if gathered is None else gathered + term
    volume[...] = gathered

    def own_part(f, carry):
        links = near_ref[f]
        for q in range(4):
            got = dot(table[:, 0:1536], one_hot(links[q : q + 1, :], 6))
            fetched[f, :, q * 256 : q * 256 + 256] = got.astype(BF16)
        return carry

    lax.fori_loop(0, 6, own_part, 0)

    for k, (copy, steps) in enumerate(copies):
        pl.when(there(-steps))(copy.wait_recv)
        high, low = split(halo[k])
        table[0:128, 1536 + k * 256 : 1792 + k * 256] = high
        table[128:256, 1536 + k * 256 : 1792 + k * 256] = low

    for load in loads[5:]:
        load.wait()

    def one_face(f, carry):
        links = near_ref[f]
        kind = kind_ref[pl.ds(f, 1), :]
        g = [
            fetched[f, :, q * 256 : q * 256 + 256]
            + dot(table[:, 1536:2048], one_hot(links[q : q + 1, :] - 1536, 2)).astype(BF16)
            for q in range(4)
        ]
        fine = dot(mortar_hi[0:960, :], g[0]) + dot(mortar_lo[0:960, :], g[0][0:128])
        coarse = fine[800:960]
        for q in range(1, 4):
            cut = slice(800 + q * 160, 960 + q * 160)
            coarse = coarse + dot(mortar_hi[cut, :], g[q]) + dot(mortar_lo[cut, :], g[q][0:128])
        outer = jnp.where(kind == 5, coarse, fine[0:160])
        for k in range(1, 5):
            outer = jnp.where(kind == k, fine[k * 160 : k * 160 + 160], outer)
        top = pl.multiple_of(f * 32, 32)
        side = jnp.where(lax.rem(f, 2) == 1, 1.0, -1.0)
        n = [normal[pl.ds(top, 32), j * 256 : j * 256 + 256] * side for j in range(3)]
        d = [
            outer[v * 32 : v * 32 + 32] - inner[pl.ds(top, 32), v * 256 : v * 256 + 256]
            for v in range(5)
        ]
        speed = speed_bound * (jnp.abs(n[0]) + jnp.abs(n[1]) + jnp.abs(n[2]))
        along = n[0] * d[1] + n[1] * d[2] + n[2] * d[3]
        excess = mean_flow[0] * n[0] + mean_flow[1] * n[1] + mean_flow[2] * n[2] - speed
        parts = [excess * d[0] + along]
        parts += [excess * d[1 + j] + n[j] * d[4] for j in range(3)]
        parts.append(excess * d[4] + along)
        for v in range(5):
            lift[pl.ds(top, 32), v * 256 : v * 256 + 256] = (0.5 * lift_scale) * parts[v]
        return carry

    lax.fori_loop(0, 6, one_face, 0)

    for k, move in enumerate(moves):
        pl.when(there(band_steps[k]))(move.wait_send)
    for copy, steps in copies:
        pl.when(there(steps))(copy.wait_send)
    high, low = split(lift[...])
    result = volume[...] + dot(pick_t[...], high) + dot(pick_t[...], low)
    for v in range(5):
        piece = result[:, v * 256 : v * 256 + 256].reshape(25, 8, 256)[:, 0:5, :]
        out_ref[v * 25 : v * 25 + 25] = -jac_ref[...] * piece


def local(
    sizes, coeffs, refine_flag, new_owner, inv_jac, metric, neighbor, mortar, export_up, export_down
):
    constants, lift_scale = operators()
    count = coeffs.shape[-1]
    elements = inv_jac.shape[-1]
    refine_hi, refine_lo, slope_hi, slope_lo, pick, pick_t, mortar_hi, mortar_lo = (
        jnp.asarray(c) for c in constants
    )
    rows = jnp.transpose(metric, (0, 2, 3, 4, 1, 5)).reshape(75, 5, 3, elements)
    jac = inv_jac.reshape(25, 5, elements)
    early = (
        coeffs.reshape(125, 5, count),
        refine_flag.reshape(1, count),
        new_owner.reshape(1, count),
        jnp.transpose(neighbor, (1, 0, 2)),
        mortar,
        export_up.reshape(1, elements),
        export_down.reshape(1, elements),
        pick,
    )
    late = (rows, refine_hi, refine_lo, slope_hi, slope_lo, pick_t, mortar_hi, mortar_lo, jac)
    vmem = pl.BlockSpec(memory_space=pltpu.VMEM)
    out = pl.pallas_call(
        functools.partial(body, sizes, lift_scale),
        out_shape=jax.ShapeDtypeStruct((125, 5, elements), F32),
        in_specs=[vmem] * len(early) + [pl.BlockSpec(memory_space=pl.ANY)] * len(late),
        out_specs=vmem,
        scratch_shapes=[pltpu.VMEM(x.shape, x.dtype) for x in late]
        + [
            pltpu.VMEM((1280, count), F32),
            pltpu.VMEM((4, 8, 1408), F32),
            pltpu.VMEM((4, 8, 1408), F32),
            pltpu.VMEM((200, 1280), F32),
            pltpu.VMEM((3, 25, 8, 768), F32),
            pltpu.VMEM((3, 200, 1280), BF16),
            pltpu.VMEM((3, 200, 1280), BF16),
            pltpu.VMEM((200, 1280), F32),
            pltpu.VMEM((192, 1280), F32),
            pltpu.VMEM((192, 768), F32),
            pltpu.VMEM((128, 1536), F32),
            pltpu.VMEM((256, 2048), BF16),
            pltpu.VMEM((2, 128, 256), F32),
            pltpu.VMEM((2, 128, 256), F32),
            pltpu.VMEM((192, 1280), F32),
            pltpu.VMEM((6, 256, 1024), BF16),
            pltpu.SemaphoreType.DMA((6,)),
            pltpu.SemaphoreType.DMA((6,)),
            pltpu.SemaphoreType.DMA((9,)),
        ],
        compiler_params=pltpu.CompilerParams(
            collective_id=0, has_side_effects=True, vmem_limit_bytes=56 * 2**20
        ),
    )(*early, *late)
    return out.reshape(5, 5, 5, 5, elements)


def solution(mesh):
    sizes = tuple(mesh.shape[axis] for axis in AXES)
    in_specs = (
        P(None, None, None, None, AXES),
        P(AXES),
        P(AXES),
        P(None, None, None, AXES),
        P(None, None, None, None, None, AXES),
        P(None, None, AXES),
        P(None, AXES),
        P(AXES),
        P(AXES),
    )
    return jax.shard_map(
        functools.partial(local, sizes),
        mesh=mesh,
        in_specs=in_specs,
        out_specs=P(None, None, None, None, AXES),
        check_vma=False,
    )
```
